32 devices in a mesh: expert: 16 (over z, y, core), tensor: 2 (over x).
Axes of the slice: x: 2, y: 2, z: 4, core: 2. Of those that a mesh axis runs over, the one named last changes fastest.
Arguments:
- attn_partial: bfloat16 [2, 256, 3584], P('tensor', 'expert'), may hold values from -4 to 4
- residual_in: bfloat16 [256, 3584], P(('expert', 'tensor')), may hold values from -6 to 6
- norm_gain: bfloat16 [3584], replicated, may hold values from 0.25 to 1.75
- w_in: bfloat16 [16, 3584, 1024], P('expert', None, 'tensor'), may hold values from -0.09375 to 0.09375
- w_out: bfloat16 [16, 1024, 3584], P('expert', 'tensor'), may hold values from -0.375 to 0.375
- routes: int32 [256, 8], P('expert'), may hold values from 0 to 15, all different within a row; in each aligned block of 16 rows (0 to 15, 16 to 31, ...) at most 16 rows name the same one
- gate_weights: float32 [256, 8], P('expert'), may hold values from 0.05 to 0.5
Outputs:
- layer_out: bfloat16 [256, 3584], P('expert')
The draws below stay inside these ranges and needn't reach their ends.
Inputs may be any that keep to these rules, and one draw needn't show every extreme that they name: `routes`: each row names 8 different experts. In each aligned block of 16 rows (the tokens of one index of expert) no expert is named by more than 16 rows, and in some block an expert is named by exactly 16 rows.
All inputs are finite; a program needn't handle non-finite values.
Results may differ from the reference program's by a relative error of at most 0.02.
Values may be sent and summed in bfloat16 or wider, within the bound.
A program may use at most 64 MiB of HBM per device.

```python
import math
import jax
import jax.numpy as jnp
import numpy as np
from jax import lax

D = 3584
H = 1024
TOP = 8
QB = 128
TOKG = 16
TOKENS = 256
EXPERTS = 16
CAP = 16
N_EXPERT = 16
N_TENSOR = 2


def level_of(own_key, shape, shards, least, top_value):
    gain = 1.0
    for dim, shards_of in shards:
        heights = jax.random.uniform(jax.random.fold_in(jax.random.fold_in(own_key, 6), dim), (shards_of,), jnp.float32, least / len(shards), top_value / len(shards))
        gain = gain * jnp.repeat(jnp.exp(heights), shape[dim] // shards_of).reshape((-1,) + (1,) * (len(shape) - 1 - dim))
    return gain


def shared_out(key, own, number, rows, count, top, most, skew):
    ranking = jax.random.permutation(key, count)
    crowded, usual = load_shares(count, rows * top, most, skew, True), load_shares(count, rows * top, most, skew, False)
    places = jnp.arange(count)

    def named(tallies, rotation):
        used = int((tallies > 0).sum())
        fixed = max(1, used // 4)
        shifted = fixed + (places - fixed + rotation * (used - fixed)) % max(1, count - fixed)
        return jnp.zeros((count,), jnp.int32).at[ranking[jnp.where(places < fixed, places, shifted)]].set(jnp.asarray(tallies, jnp.int32))

    tallies = jnp.where(number % 4 == 0, named(crowded, number // 4), named(usual, number - number // 4 - 1))
    mixed = jax.random.permutation(jax.random.fold_in(own, 3), count)
    donor, taker = mixed[0:count // 2 * 2:2], mixed[1:count // 2 * 2:2]
    margin = jnp.minimum(tallies[donor] - 1, most - tallies[taker]) // 2
    margin = jnp.where((donor == ranking[0]) | (taker == ranking[0]) | (tallies[taker] == 0), 0, jnp.maximum(margin, 0))
    shifted = jax.random.randint(jax.random.fold_in(own, 4), (count // 2,), 0, 1 << 20) % (margin + 1)
    tallies = tallies.at[donor].add(-shifted).at[taker].add(shifted)
    items = jnp.searchsorted(jnp.cumsum(tallies), jnp.arange(rows * top), side="right").astype(jnp.int32)
    table = items.reshape(top, rows).T
    table = table[jax.random.permutation(jax.random.fold_in(own, 1), rows)]
    rotation = jax.random.randint(jax.random.fold_in(own, 2), (rows, 1), 0, top)
    return jnp.take_along_axis(table, (jnp.arange(top)[None, :] + rotation) % top, axis=1)


def load_shares(count, total, most, skew, full):
    loads = [(1 << 20) // math.isqrt(grade ** skew) + 1 for grade in range(1, count + 1)]
    largest = most if full else min(most, max(-(-total // count), total * loads[0] // sum(loads)))
    least = 1 if total - largest >= count - 1 else 0
    given, surplus = [largest] + [least] * (count - 1), total - largest - least * (count - 1)
    while surplus > 0:
        free = [i for i in range(1, count) if given[i] < largest] or [i for i in range(1, count) if given[i] < most]
        pool, remaining = sum([loads[i] for i in free]), surplus
        for i in free:
            more = min(most - given[i], max(1, remaining * loads[i] // pool), surplus)
            given[i] = given[i] + more
            surplus = surplus - more
    return np.array(given)


def bell_draw(own_key, shape, spread, most, cuts=(), held_as=jnp.bfloat16):
    values = spread * jax.random.normal(own_key, shape, jnp.float32)
    if cuts:
        values = values * level_of(own_key, shape, cuts, -0.22, 0.18)
    return jnp.clip(values, -most, most).astype(held_as)


def setup_inputs(seed: int = 0) -> dict:
    seeds = jax.random.split(jax.random.key(seed), 8)
    attn_partial = bell_draw(seeds[0], (N_TENSOR, TOKENS, D), 0.5, 4.0, ((0, 2), (1, 16)))
    residual_in = bell_draw(seeds[1], (TOKENS, D), 1.0, 6.0, ((0, 32),))
    norm_gain = jnp.clip(1.0 + 0.15 * jax.random.normal(seeds[2], (D,), jnp.float32), 0.25, 1.75).astype(jnp.bfloat16)
    w_in = bell_draw(seeds[3], (EXPERTS, D, H), D ** -0.5, 0.09375, ((0, 16), (2, 2)))
    w_out = bell_draw(seeds[4], (EXPERTS, H, D), (H // 4) ** -0.5, 0.375, ((0, 16), (1, 2)))
    routes_keys = jax.random.split(jax.random.fold_in(seeds[5], 1), TOKENS // TOKG)
    routes_turns = jax.random.permutation(jax.random.fold_in(seeds[5], 3), TOKENS // TOKG)
    routes = jax.vmap(lambda own, number: shared_out(jax.random.fold_in(seeds[5], 2), own, number, TOKG, EXPERTS, TOP, CAP, 2))(routes_keys, routes_turns).reshape((TOKENS, TOP))
    gate_weights = jnp.clip(0.05 + 0.45 * jax.random.uniform(seeds[6], (TOKENS, TOP), jnp.float32) ** level_of(seeds[6], (TOKENS, TOP), ((0, 16),), -0.2, 0.2), 0.05, 0.5)
    return {"attn_partial": attn_partial, "residual_in": residual_in, "norm_gain": norm_gain, "w_in": w_in, "w_out": w_out, "routes": routes, "gate_weights": gate_weights}


def slot_tables(routes):
    pairs = routes.reshape(N_EXPERT, TOKG * TOP)
    onehot = (pairs[:, :, None] == jnp.arange(EXPERTS, dtype=jnp.int32)[None, None, :]).astype(jnp.int32)
    earlier = jnp.cumsum(onehot, axis=1) - onehot
    slot_index = lax.optimization_barrier(jnp.sum(earlier * onehot, axis=2)).astype(jnp.int32)
    target = (pairs * CAP + slot_index).astype(jnp.int32)
    group_ids = jnp.broadcast_to(jnp.arange(N_EXPERT, dtype=jnp.int32)[:, None], target.shape)
    pair_ids = jnp.arange(TOKENS * TOP, dtype=jnp.int32).reshape(N_EXPERT, TOKG * TOP)
    table = jnp.full((N_EXPERT, EXPERTS * CAP), -1, jnp.int32)
    return table.at[group_ids, target].set(pair_ids)

def reference(attn_partial, residual_in, norm_gain, w_in, w_out, routes, gate_weights):
    attention = lax.optimization_barrier(jnp.sum(attn_partial.astype(jnp.float32), axis=0))
    residual = (residual_in.astype(jnp.float32) + attention).astype(jnp.bfloat16)
    stream = residual.astype(jnp.float32)
    rms_value = jnp.sqrt(lax.optimization_barrier(jnp.mean(stream * stream, axis=1, keepdims=True)) + 1e-06)
    normed = stream / rms_value * norm_gain.astype(jnp.float32)
    blocks = normed.reshape(TOKENS, D // QB, QB)
    block_scale = (lax.optimization_barrier(jnp.max(jnp.abs(blocks), axis=2)) + 1e-06).astype(jnp.bfloat16)
    scale_wide = block_scale.astype(jnp.float32)[:, :, None]
    quantized = lax.optimization_barrier((blocks / scale_wide).astype(jnp.bfloat16))
    expert_input = (quantized.astype(jnp.float32) * scale_wide).reshape(TOKENS, D).astype(jnp.bfloat16)
    table = slot_tables(routes)
    gate_flat = gate_weights.reshape(-1).astype(jnp.float32)
    quarter = H // N_TENSOR

    def one_expert(index, total):
        slot_pairs = lax.dynamic_slice_in_dim(table, index * CAP, CAP, 1).reshape(-1)
        filled = slot_pairs >= 0
        safe_pairs = jnp.maximum(slot_pairs, 0)
        token_ids = (safe_pairs // TOP).astype(jnp.int32)
        row_block = jnp.where(filled[:, None], expert_input[token_ids], jnp.zeros((), jnp.bfloat16))
        weights_in = w_in[index]
        weights_out = w_out[index]
        hidden = jax.nn.silu(jnp.dot(row_block, weights_in, preferred_element_type=jnp.float32)).astype(jnp.bfloat16)
        summed = jnp.zeros((row_block.shape[0], D), jnp.float32)
        for lane in range(N_TENSOR):
            term = jnp.dot(hidden[:, lane * quarter:(lane + 1) * quarter], weights_out[lane * quarter:(lane + 1) * quarter], preferred_element_type=jnp.float32).astype(jnp.bfloat16)
            summed = summed + lax.optimization_barrier(term).astype(jnp.float32)
        expert_out = lax.optimization_barrier(summed.astype(jnp.bfloat16)).astype(jnp.float32)
        weight = jnp.where(filled, gate_flat[safe_pairs], jnp.zeros((), jnp.float32))
        return total.at[token_ids].add(expert_out * weight[:, None])
    mixture = lax.fori_loop(0, EXPERTS, one_expert, jnp.zeros((TOKENS, D), jnp.float32))
    return (stream + mixture).astype(jnp.bfloat16)
```

```python
import jax
import jax.numpy as jnp
from jax import lax
from jax.sharding import PartitionSpec as P

QB = 128


EPSILON = 1e-06


def capacity(group_tokens, top_count, expert_count):
    return min(group_tokens, max(4, 2 * group_tokens * top_count // expert_count))


def own_rows(attention, residual_in, norm_gain):
    model_width = residual_in.shape[1]
    block_count = model_width // QB
    residual = (residual_in.astype(jnp.float32) + attention).astype(jnp.bfloat16)
    stream = residual.astype(jnp.float32)
    rms_value = jnp.sqrt(jnp.mean(stream * stream, axis=1, keepdims=True) + EPSILON)
    normed = stream / rms_value * norm_gain.astype(jnp.float32)
    blocks = normed.reshape(-1, block_count, QB)
    block_scale = (jnp.max(jnp.abs(blocks), axis=2) + EPSILON).astype(jnp.bfloat16)
    wide = block_scale.astype(jnp.float32)[:, :, None]
    quantized = (blocks / wide).astype(jnp.bfloat16)
    expert_input = (quantized.astype(jnp.float32) * wide).astype(jnp.bfloat16)
    return residual, expert_input.reshape(-1, model_width)


def dense_gates(routes, gate_weights, expert_count):
    chosen = routes[:, :, None] == jnp.arange(expert_count, dtype=jnp.int32)
    return jnp.sum(jnp.where(chosen, gate_weights[:, :, None], 0.0), axis=1)


def dense_shards(attn_partial, residual_in, norm_gain, w_in, w_out, routes, gate_weights):
    model_width = residual_in.shape[1]
    expert_count = lax.axis_size("expert")
    attention = lax.psum_scatter(
        attn_partial[0], "tensor", scatter_dimension=0, tiled=True
    ).astype(jnp.float32)
    residual, expert_input = own_rows(attention, residual_in, norm_gain)
    own_count = residual.shape[0]
    gates = dense_gates(routes, gate_weights, expert_count)
    gates = lax.dynamic_slice_in_dim(gates, lax.axis_index("tensor") * own_count, own_count, 0)
    high = gates.astype(jnp.bfloat16)
    middle = (gates - high.astype(jnp.float32)).astype(jnp.bfloat16)
    rest = gates - high.astype(jnp.float32) - middle.astype(jnp.float32)
    pieces = jnp.concatenate([high, middle, rest.astype(jnp.bfloat16)], axis=1)
    pieces = jnp.pad(pieces, ((0, 0), (0, QB - pieces.shape[1])))
    packed = jnp.concatenate([expert_input, pieces], axis=1)
    everything = lax.all_gather(packed, ("expert", "tensor"), axis=0, tiled=True)
    rows, codes = everything[:, :model_width], everything[:, model_width:]
    mine = lax.axis_index("expert")
    lane = jnp.arange(QB, dtype=jnp.int32)[None, :]
    own_lane = (lane < 3 * expert_count) & (lane % expert_count == mine)
    gate = jnp.sum(jnp.where(own_lane, codes.astype(jnp.float32), 0.0), axis=1, keepdims=True)
    hidden = jax.nn.silu(jnp.dot(rows, w_in[0], preferred_element_type=jnp.float32)).astype(
        jnp.bfloat16
    )
    partial_value = jnp.dot(hidden, w_out[0], preferred_element_type=jnp.float32)
    weighted = (partial_value * gate).astype(jnp.bfloat16)
    mixture = lax.psum_scatter(
        weighted, ("expert", "tensor"), scatter_dimension=0, tiled=True
    ).astype(jnp.float32)
    out_part = (residual.astype(jnp.float32) + mixture).astype(jnp.bfloat16)
    return lax.all_gather(out_part, "tensor", axis=0, tiled=True)


def shards(attn_partial, residual_in, norm_gain, w_in, w_out, routes, gate_weights):
    group_tokens, top_count = routes.shape
    model_width = residual_in.shape[1]
    expert_count = lax.axis_size("expert")
    slot_count = capacity(group_tokens, top_count, expert_count)
    block_count = model_width // QB
    if slot_count == group_tokens:
        return dense_shards(
            attn_partial, residual_in, norm_gain, w_in, w_out, routes, gate_weights
        )
    attention = lax.psum_scatter(
        attn_partial[0].astype(jnp.float32).astype(jnp.bfloat16),
        "tensor",
        scatter_dimension=0,
        tiled=True,
    ).astype(jnp.float32)
    residual = (residual_in.astype(jnp.float32) + attention).astype(jnp.bfloat16)
    stream = residual.astype(jnp.float32)
    rms_value = jnp.sqrt(jnp.mean(stream * stream, axis=1, keepdims=True) + EPSILON)
    normed = stream / rms_value * norm_gain.astype(jnp.float32)
    blocks = normed.reshape(-1, block_count, QB)
    block_scale = (jnp.max(jnp.abs(blocks), axis=2) + EPSILON).astype(jnp.bfloat16)
    quantized = (
        (blocks / block_scale.astype(jnp.float32)[:, :, None])
        .astype(jnp.bfloat16)
        .reshape(-1, model_width)
    )
    group_quant, group_scale, group_resid = (
        lax.all_gather(quantized, "tensor", axis=0, tiled=True),
        lax.all_gather(block_scale, "tensor", axis=0, tiled=True),
        lax.all_gather(residual, "tensor", axis=0, tiled=True),
    )
    pair_expert = routes.reshape(-1)
    order = jnp.arange(pair_expert.shape[0], dtype=jnp.int32)
    before = (pair_expert[:, None] == pair_expert[None, :]) & (order[None, :] < order[:, None])
    slot_index = jnp.sum(before.astype(jnp.int32), axis=1)
    target = pair_expert * slot_count + slot_index
    pair_total = group_tokens * top_count
    slot_table = (
        jnp.full((expert_count * slot_count,), -1, jnp.int32)
        .at[target]
        .set(jnp.arange(pair_total, dtype=jnp.int32))
    )
    slot_table = slot_table.reshape(expert_count, slot_count)
    filled = slot_table >= 0
    token_ids = jnp.maximum(slot_table, 0) // top_count
    row_block = jnp.where(filled[:, :, None], group_quant[token_ids], jnp.zeros((), jnp.bfloat16))
    scales = jnp.where(filled[:, :, None], group_scale[token_ids], jnp.zeros((), jnp.bfloat16))
    recv_rows, recv_scales = (
        lax.all_to_all(row_block, "expert", split_axis=0, concat_axis=0, tiled=True),
        lax.all_to_all(scales, "expert", split_axis=0, concat_axis=0, tiled=True),
    )
    sources = recv_rows.shape[0]
    widened = recv_rows.reshape(sources, slot_count, block_count, QB).astype(jnp.float32)
    expert_input = (
        (widened * recv_scales.astype(jnp.float32)[:, :, :, None])
        .reshape(sources * slot_count, model_width)
        .astype(jnp.bfloat16)
    )
    hidden = jax.nn.silu(jnp.dot(expert_input, w_in[0], preferred_element_type=jnp.float32)).astype(
        jnp.bfloat16
    )
    partial_value = jnp.dot(hidden, w_out[0], preferred_element_type=jnp.float32).reshape(
        sources, slot_count, model_width
    )
    summed = lax.psum_scatter(
        partial_value.astype(jnp.bfloat16), "tensor", scatter_dimension=2, tiled=True
    )
    returned = lax.all_to_all(summed, "expert", split_axis=0, concat_axis=0, tiled=True)
    quarter = returned.shape[2]
    flat_back = returned.reshape(expert_count * slot_count, quarter)
    picked = flat_back[target].astype(jnp.float32) * gate_weights.reshape(-1)[:, None]
    mixture = jnp.sum(picked.reshape(group_tokens, top_count, quarter), axis=1)
    resid_part = lax.dynamic_slice_in_dim(
        group_resid, lax.axis_index("tensor") * quarter, quarter, 1
    )
    out_part = (resid_part.astype(jnp.float32) + mixture).astype(jnp.bfloat16)
    return lax.all_gather(out_part, "tensor", axis=1, tiled=True)


def solution(mesh):
    return jax.shard_map(
        shards,
        mesh=mesh,
        in_specs=(
            P("tensor", "expert", None),
            P(("expert", "tensor"), None),
            P(),
            P("expert", None, "tensor"),
            P("expert", "tensor", None),
            P("expert", None),
            P("expert", None),
        ),
        out_specs=P("expert", None),
        check_vma=False,
    )
```

```python
import functools

import jax
import jax.numpy as jnp
from jax import lax
from jax.experimental import pallas as pl
from jax.experimental.pallas import tpu as pltpu
from jax.sharding import PartitionSpec as P

QB = 128


EPSILON = 1e-06


def capacity(group_tokens, top_count, expert_count):
    return min(group_tokens, max(4, 2 * group_tokens * top_count // expert_count))


MESH = pl.DeviceIdType.MESH


def place():
    e, t = lax.axis_index("expert"), lax.axis_index("tensor")
    return e // 4, (e // 2) % 2, e % 2, t


def greet(depth):
    z, y, c, t = place()
    others = [(lax.rem(z + k, depth) * 4 + y * 2 + c, t) for k in range(1, depth)]
    others += [
        (z * 4 + (1 - y) * 2 + c, t),
        (z * 4 + y * 2 + 1 - c, t),
        (z * 4 + y * 2 + c, 1 - t),
    ]
    barrier = pltpu.get_barrier_semaphore()
    for other in others:
        pl.semaphore_signal(barrier, inc=1, device_id=other, device_id_type=MESH)
    pl.semaphore_wait(barrier, len(others))


def send(source, target, sems, lane, k, other):
    copy = pltpu.make_async_remote_copy(
        src_ref=source,
        dst_ref=target,
        send_sem=sems.at[0, lane, k],
        recv_sem=sems.at[1, lane, k],
        device_id=other,
        device_id_type=MESH,
    )
    copy.start()
    return copy


def gather_kernel(
    depth, cut, attn, resid_in, gain, codes, resid, rows, got, sems
):
    z, y, c, t = place()
    width = resid_in.shape[1]
    beside_x = (z * 4 + y * 2 + c, 1 - t)
    beside_y = (z * 4 + (1 - y) * 2 + c, t)
    beside_c = (z * 4 + y * 2 + 1 - c, t)
    greet(depth)
    first = send(attn.at[1 - t], got, sems, 0, 0, beside_x)
    rows[z, y, c, t, :, width:] = codes[...]
    first.wait_recv()
    attention = attn[t].astype(jnp.float32) + got[...].astype(jnp.float32)
    residual = (resid_in[...].astype(jnp.float32) + attention).astype(jnp.bfloat16)
    resid[...] = residual
    stream = residual.astype(jnp.float32)
    rms_value = jnp.sqrt(jnp.mean(stream * stream, axis=1, keepdims=True) + EPSILON)
    normed = stream / rms_value * gain[...].astype(jnp.float32)
    for b in range(width // QB):
        block = normed[:, b * QB : (b + 1) * QB]
        top = jnp.max(jnp.abs(block), axis=1, keepdims=True)
        scale = (top + EPSILON).astype(jnp.bfloat16).astype(jnp.float32)
        quantized = (block / scale).astype(jnp.bfloat16).astype(jnp.float32)
        rows[z, y, c, t, :, b * QB : (b + 1) * QB] = (quantized * scale).astype(jnp.bfloat16)
    left, right = pl.ds(0, cut), pl.ds(cut, rows.shape[5] - cut)
    along = []
    for k in range(1, depth):
        other = (lax.rem(z + k, depth) * 4 + y * 2 + c, t)
        own = rows.at[z, y, c, t]
        along.append(send(own, own, sems, 1, k, other))
    ring = [lax.rem(z - k + depth, depth) for k in range(depth)]
    second, third, last = [], [], []
    for k in range(depth):
        if k:
            along[k - 1].wait_recv()
        one = rows.at[ring[k], y, c, t, :, left]
        two = rows.at[ring[k], y, c, t, :, right]
        second.append(
            (
                send(one, one, sems, 2, k, beside_y),
                send(two, two, sems, 3, k, beside_x),
            )
        )
    for k in range(depth):
        second[k][0].wait_recv()
        one = rows.at[ring[k], :, c, t, :, left]
        third.append(send(one, one, sems, 4, k, beside_x))
        second[k][1].wait_recv()
        two = rows.at[ring[k], y, c, :, :, right]
        third.append(send(two, two, sems, 5, k, beside_y))
    for k in range(depth):
        third[2 * k].wait_recv()
        third[2 * k + 1].wait_recv()
        plane = rows.at[ring[k], :, c]
        last.append(send(plane, plane, sems, 6, k, beside_c))
    for copy in last:
        copy.wait_recv()
    for copy in [first] + along + [p for pair in second for p in pair] + third + last:
        copy.wait_send()


def add(one, two):
    return one.astype(jnp.float32) + two.astype(jnp.float32)


def reduce_kernel(
    depth, cut, terms, resid, out, r1, s1, ra, rb, sa, sb, qa, qb, f, rz, sems
):
    z, y, c, t = place()
    bf16 = jnp.bfloat16
    beside_x = (z * 4 + y * 2 + c, 1 - t)
    beside_y = (z * 4 + (1 - y) * 2 + c, t)
    beside_c = (z * 4 + y * 2 + 1 - c, t)
    width = resid.shape[1]
    left, right = pl.ds(0, cut), pl.ds(cut, width - cut)
    greet(depth)
    steps = list(range(1, depth)) + [0]
    ring = [lax.rem(z + k, depth) for k in range(depth)]
    one, two, three, four, five, six = {}, {}, {}, {}, {}, {}
    for k in steps:
        one[k] = send(terms.at[ring[k], :, 1 - c], r1.at[k], sems, 0, k, beside_c)
    for k in steps:
        one[k].wait_recv()
        for i in range(2):
            for j in range(2):
                s1[k, i, j] = add(terms[ring[k], i, c, j], r1[k, i, j]).astype(bf16)
        two[k] = send(s1.at[k, :, 1 - t, :, left], ra.at[k], sems, 1, k, beside_x)
        three[k] = send(s1.at[k, 1 - y, :, :, right], rb.at[k], sems, 2, k, beside_y)
    for k in steps:
        two[k].wait_recv()
        sa[k] = add(s1[k, :, t, :, :cut], ra[k]).astype(bf16)
        four[k] = send(sa.at[k, 1 - y], qa.at[k], sems, 3, k, beside_y)
        three[k].wait_recv()
        sb[k] = add(s1[k, y, :, :, cut:], rb[k]).astype(bf16)
        five[k] = send(sb.at[k, 1 - t], qb.at[k], sems, 4, k, beside_x)
    for k in steps:
        four[k].wait_recv()
        f[k, :, :cut] = add(sa[k, y], qa[k]).astype(bf16)
        five[k].wait_recv()
        f[k, :, cut:] = add(sb[k, t], qb[k]).astype(bf16)
        if k:
            six[k] = send(f.at[k], rz.at[k], sems, 5, k, (ring[k] * 4 + y * 2 + c, t))
    total = add(resid[...], f[0])
    for k in range(1, depth):
        six[k].wait_recv()
        total = total + rz[k].astype(jnp.float32)
    out[t] = total.astype(bf16)
    end = send(out.at[t], out.at[t], sems, 6, 0, beside_x)
    end.wait_recv()
    for group in (one, two, three, four, five, six, {0: end}):
        for k in group:
            group[k].wait_send()


def in_vmem(count):
    return [pl.BlockSpec(memory_space=pltpu.VMEM)] * count


def gather_rows(attn, residual_in, norm_gain, codes):
    own, width = residual_in.shape
    depth = lax.axis_size("expert") // 4
    packed = width + codes.shape[1]
    cut = (packed // QB + 1) // 2 * QB
    bf16 = jnp.bfloat16
    return pl.pallas_call(
        functools.partial(gather_kernel, depth, cut),
        out_shape=(
            jax.ShapeDtypeStruct((own, width), bf16),
            jax.ShapeDtypeStruct((depth, 2, 2, 2, own, packed), bf16),
        ),
        in_specs=in_vmem(4),
        out_specs=tuple(in_vmem(2)),
        scratch_shapes=[
            pltpu.VMEM((own, width), bf16),
            pltpu.SemaphoreType.DMA((2, 7, depth)),
        ],
        compiler_params=pltpu.CompilerParams(
            collective_id=0, has_side_effects=True, vmem_limit_bytes=16 << 20
        ),
        cost_estimate=pl.CostEstimate(flops=10**9, bytes_accessed=60 * 10**6, transcendentals=0),
    )(attn.reshape(2, own, width), residual_in, norm_gain.reshape(1, width), codes)


def reduce_rows(terms, residual):
    own, width = residual.shape
    depth = terms.shape[0]
    cut = (width // QB + 1) // 2 * QB
    bf16 = jnp.bfloat16
    return pl.pallas_call(
        functools.partial(reduce_kernel, depth, cut),
        out_shape=jax.ShapeDtypeStruct((2, own, width), bf16),
        in_specs=in_vmem(2),
        out_specs=in_vmem(1)[0],
        scratch_shapes=[
            pltpu.VMEM((depth, 2, 2, own, width), bf16),
            pltpu.VMEM((depth, 2, 2, own, width), bf16),
            pltpu.VMEM((depth, 2, own, cut), bf16),
            pltpu.VMEM((depth, 2, own, width - cut), bf16),
            pltpu.VMEM((depth, 2, own, cut), bf16),
            pltpu.VMEM((depth, 2, own, width - cut), bf16),
            pltpu.VMEM((depth, own, cut), bf16),
            pltpu.VMEM((depth, own, width - cut), bf16),
            pltpu.VMEM((depth, own, width), bf16),
            pltpu.VMEM((depth, own, width), bf16),
            pltpu.SemaphoreType.DMA((2, 7, depth)),
        ],
        compiler_params=pltpu.CompilerParams(
            collective_id=1, has_side_effects=True, vmem_limit_bytes=24 << 20
        ),
    )(terms, residual)


def dense_gates(routes, gate_weights, expert_count):
    chosen = routes[:, :, None] == jnp.arange(expert_count, dtype=jnp.int32)
    return jnp.sum(jnp.where(chosen, gate_weights[:, :, None], 0.0), axis=1)


def dense_shards(attn_partial, residual_in, norm_gain, w_in, w_out, routes, gate_weights):
    model_width = residual_in.shape[1]
    expert_count = lax.axis_size("expert")
    own_count = residual_in.shape[0]
    gates = dense_gates(routes, gate_weights, expert_count)
    gates = lax.dynamic_slice_in_dim(gates, lax.axis_index("tensor") * own_count, own_count, 0)
    high = gates.astype(jnp.bfloat16)
    middle = (gates - high.astype(jnp.float32)).astype(jnp.bfloat16)
    rest = gates - high.astype(jnp.float32) - middle.astype(jnp.float32)
    pieces = jnp.concatenate([high, middle, rest.astype(jnp.bfloat16)], axis=1)
    pieces = jnp.pad(pieces, ((0, 0), (0, QB - pieces.shape[1])))
    residual, everything = gather_rows(attn_partial[0], residual_in, norm_gain, pieces)
    shape = everything.shape
    everything = everything.reshape(-1, shape[-1])
    rows, codes = everything[:, :model_width], everything[:, model_width:]
    mine = lax.axis_index("expert")
    lane = jnp.arange(QB, dtype=jnp.int32)[None, :]
    own_lane = (lane < 3 * expert_count) & (lane % expert_count == mine)
    gate = jnp.sum(jnp.where(own_lane, codes.astype(jnp.float32), 0.0), axis=1, keepdims=True)
    hidden = jax.nn.silu(jnp.dot(rows, w_in[0], preferred_element_type=jnp.float32)).astype(
        jnp.bfloat16
    )
    partial_value = jnp.dot(hidden, w_out[0], preferred_element_type=jnp.float32)
    weighted = (partial_value * gate).astype(jnp.bfloat16)
    out = reduce_rows(weighted.reshape(shape[:-1] + (model_width,)), residual)
    return out.reshape(-1, model_width)


def shards(attn_partial, residual_in, norm_gain, w_in, w_out, routes, gate_weights):
    group_tokens, top_count = routes.shape
    model_width = residual_in.shape[1]
    expert_count = lax.axis_size("expert")
    slot_count = capacity(group_tokens, top_count, expert_count)
    block_count = model_width // QB
    if slot_count == group_tokens and expert_count == 16 and lax.axis_size("tensor") == 2:
        return dense_shards(
            attn_partial, residual_in, norm_gain, w_in, w_out, routes, gate_weights
        )
    attention = lax.psum_scatter(
        attn_partial[0].astype(jnp.float32).astype(jnp.bfloat16),
        "tensor",
        scatter_dimension=0,
        tiled=True,
    ).astype(jnp.float32)
    residual = (residual_in.astype(jnp.float32) + attention).astype(jnp.bfloat16)
    stream = residual.astype(jnp.float32)
    rms_value = jnp.sqrt(jnp.mean(stream * stream, axis=1, keepdims=True) + EPSILON)
    normed = stream / rms_value * norm_gain.astype(jnp.float32)
    blocks = normed.reshape(-1, block_count, QB)
    block_scale = (jnp.max(jnp.abs(blocks), axis=2) + EPSILON).astype(jnp.bfloat16)
    quantized = (
        (blocks / block_scale.astype(jnp.float32)[:, :, None])
        .astype(jnp.bfloat16)
        .reshape(-1, model_width)
    )
    group_quant, group_scale, group_resid = (
        lax.all_gather(quantized, "tensor", axis=0, tiled=True),
        lax.all_gather(block_scale, "tensor", axis=0, tiled=True),
        lax.all_gather(residual, "tensor", axis=0, tiled=True),
    )
    pair_expert = routes.reshape(-1)
    order = jnp.arange(pair_expert.shape[0], dtype=jnp.int32)
    before = (pair_expert[:, None] == pair_expert[None, :]) & (order[None, :] < order[:, None])
    slot_index = jnp.sum(before.astype(jnp.int32), axis=1)
    target = pair_expert * slot_count + slot_index
    pair_total = group_tokens * top_count
    slot_table = (
        jnp.full((expert_count * slot_count,), -1, jnp.int32)
        .at[target]
        .set(jnp.arange(pair_total, dtype=jnp.int32))
    )
    slot_table = slot_table.reshape(expert_count, slot_count)
    filled = slot_table >= 0
    token_ids = jnp.maximum(slot_table, 0) // top_count
    row_block = jnp.where(filled[:, :, None], group_quant[token_ids], jnp.zeros((), jnp.bfloat16))
    scales = jnp.where(filled[:, :, None], group_scale[token_ids], jnp.zeros((), jnp.bfloat16))
    recv_rows, recv_scales = (
        lax.all_to_all(row_block, "expert", split_axis=0, concat_axis=0, tiled=True),
        lax.all_to_all(scales, "expert", split_axis=0, concat_axis=0, tiled=True),
    )
    sources = recv_rows.shape[0]
    widened = recv_rows.reshape(sources, slot_count, block_count, QB).astype(jnp.float32)
    expert_input = (
        (widened * recv_scales.astype(jnp.float32)[:, :, :, None])
        .reshape(sources * slot_count, model_width)
        .astype(jnp.bfloat16)
    )
    hidden = jax.nn.silu(jnp.dot(expert_input, w_in[0], preferred_element_type=jnp.float32)).astype(
        jnp.bfloat16
    )
    partial_value = jnp.dot(hidden, w_out[0], preferred_element_type=jnp.float32).reshape(
        sources, slot_count, model_width
    )
    summed = lax.psum_scatter(
        partial_value.astype(jnp.bfloat16), "tensor", scatter_dimension=2, tiled=True
    )
    returned = lax.all_to_all(summed, "expert", split_axis=0, concat_axis=0, tiled=True)
    quarter = returned.shape[2]
    flat_back = returned.reshape(expert_count * slot_count, quarter)
    picked = flat_back[target].astype(jnp.float32) * gate_weights.reshape(-1)[:, None]
    mixture = jnp.sum(picked.reshape(group_tokens, top_count, quarter), axis=1)
    resid_part = lax.dynamic_slice_in_dim(
        group_resid, lax.axis_index("tensor") * quarter, quarter, 1
    )
    out_part = (resid_part.astype(jnp.float32) + mixture).astype(jnp.bfloat16)
    return lax.all_gather(out_part, "tensor", axis=1, tiled=True)


def solution(mesh):
    return jax.shard_map(
        shards,
        mesh=mesh,
        in_specs=(
            P("tensor", "expert", None),
            P(("expert", "tensor"), None),
            P(),
            P("expert", None, "tensor"),
            P("expert", "tensor", None),
            P("expert", None),
            P("expert", None),
        ),
        out_specs=P("expert", None),
        check_vma=False,
    )
```
